32 devices in a mesh: group: 2 (over y), req: 4 (over z), tensor: 4 (over x, core).
Axes of the slice: x: 2, y: 2, z: 4, core: 2. Of those that a mesh axis runs over, the one named last changes fastest.
Arguments:
- hidden: bfloat16 [256, 28672], P(('group', 'req')), parts along dimension 0, may hold values from -6 to 6
- down_weight: bfloat16 [28672, 8192], P('req', 'tensor'), may hold values from -0.03125 to 0.03125
- adapter_input_weight: bfloat16 [8, 64, 28672], P('req', None, 'tensor'), may hold values from -0.03125 to 0.03125
- adapter_output_weight: bfloat16 [8, 64, 8192], P('req', None, 'tensor'), may hold values from -0.75 to 0.75
- adapter_storage_index: int32 [16], P('group'), parts along dimension 0, may hold values from 0 to 7, as said below
- row_adapter_index: int32 [256], P(('group', 'req')), parts along dimension 0, may hold values from 0 to 7, as said below
Outputs:
- mixed: bfloat16 [256, 8192], P(('group', 'req'), 'tensor'), parts along dimension 0
The draws below stay inside these ranges and needn't reach their ends.
There are 2 independent parts, one for each index of `group`. The reference program is written for one: setup_inputs(seed, part) draws one part's arguments, and reference() takes and returns one part's arrays. A program takes and returns all parts, laid end to end along the dimension named above; an argument that names none is the same for every part. Nothing has to cross between parts.
Inputs may be any that keep to these rules, and one draw needn't show every extreme that they name: `adapter_storage_index`: each adapter has its own storage index. `row_adapter_index`: among the 32 rows of one index of req, at most 24 name adapters whose storage index // 2 is the same; in every draw, each index of req has exactly 24 rows for some one owner, which need not be the same owner for different indices.
All inputs are finite; a program needn't handle non-finite values.
Results may differ from the reference program's by a relative error of at most 0.005.
Values may be sent and summed in bfloat16 or wider, within the bound.
A program may use at most 128 MiB of HBM per device.

```python
import jax
import jax.numpy as jnp
from jax import lax

EMBEDDING_WIDTH = 8192
HIDDEN_UNITS = 28672
ADAPTER_RANK = 64
ADP_DEV = 2
ROW_DEV = 32
ROWS = 128
ADAPTER_TOTAL = 8
CAP = 24
N_REQ = 4


def shared_table(key):
    return jax.random.permutation(jax.random.fold_in(key, 17), ADAPTER_TOTAL).astype(jnp.int32)


def draw_adapter_storage_index(key, part):
    return shared_table(key)


def draw_row_adapter_index(key, part):
    table = shared_table(key)
    key = jax.random.fold_in(key, 3)
    major_key, ranking_key, order_key, pick_key = jax.random.split(key, 4)
    position_total = N_REQ * CAP
    position_owner = jnp.arange(position_total, dtype=jnp.int32) // CAP
    largest_share = jax.random.randint(major_key, (N_REQ,), 0, N_REQ)
    extra_credit = jnp.where(position_owner[None, :] == largest_share[:, None], 4096 * position_total, 0)
    position_score = jax.random.randint(ranking_key, (N_REQ, position_total), 0, 4096) * position_total + jnp.arange(position_total, dtype=jnp.int32)[None, :] + extra_credit
    ranked = jnp.argsort(-position_score, axis=1)
    taken = position_owner[ranked[:, :ROW_DEV]]
    position = jax.vmap(lambda k: jax.random.permutation(k, ROW_DEV))(jax.random.split(order_key, N_REQ))
    owner = jnp.take_along_axis(taken, position, axis=1)
    pick = jax.random.randint(pick_key, (N_REQ, ROW_DEV), 0, ADP_DEV)
    storage = owner * ADP_DEV + pick
    inverse = jnp.argsort(table)
    return inverse[storage.reshape(-1)].astype(jnp.int32)


def block_scale(own_key, dims, shards, smallest, high):
    gain = 1.0
    for axis_at, shards_of in shards:
        steps = jax.random.uniform(jax.random.fold_in(jax.random.fold_in(own_key, 6), axis_at), (shards_of,), jnp.float32, smallest / len(shards), high / len(shards))
        gain = gain * jnp.repeat(jnp.exp(steps), dims[axis_at] // shards_of).reshape((-1,) + (1,) * (len(dims) - 1 - axis_at))
    return gain


def scatter_about(stream_key, extent, scale, most, cuts=(), kind=jnp.bfloat16):
    values = scale * jax.random.normal(stream_key, extent, jnp.float32)
    if cuts:
        values = values * block_scale(stream_key, extent, cuts, -0.22, 0.18)
    return jnp.clip(values, -most, most).astype(kind)


def setup_inputs(seed: int = 0, part: int = 0) -> dict:
    key_list = jax.random.split(jax.random.key(seed), 7)
    part_splits = jax.random.split(jax.random.fold_in(key_list[6], part), 7)
    return {
        "hidden": scatter_about(part_splits[0], (ROWS, HIDDEN_UNITS), 1.0, 6.0, ((0, 4),)),
        "down_weight": scatter_about(key_list[1], (HIDDEN_UNITS, EMBEDDING_WIDTH), HIDDEN_UNITS ** -0.5, 0.03125, ((0, 4), (1, 4))),
        "adapter_input_weight": scatter_about(key_list[2], (ADAPTER_TOTAL, ADAPTER_RANK, HIDDEN_UNITS), HIDDEN_UNITS ** -0.5, 0.03125, ((0, 4), (2, 4))),
        "adapter_output_weight": scatter_about(key_list[3], (ADAPTER_TOTAL, ADAPTER_RANK, EMBEDDING_WIDTH), ADAPTER_RANK ** -0.5, 0.75, ((0, 4), (2, 4))),
        "adapter_storage_index": draw_adapter_storage_index(jax.random.fold_in(jax.random.fold_in(key_list[6], part), 71), part),
        "row_adapter_index": draw_row_adapter_index(jax.random.fold_in(jax.random.fold_in(key_list[6], part), 71), part),
    }


def reference(hidden, down_weight, adapter_input_weight, adapter_output_weight, adapter_storage_index, row_adapter_index):
    base = jnp.dot(hidden, down_weight, preferred_element_type=jnp.float32)
    storage = adapter_storage_index[row_adapter_index]

    def inner_update(total, loop_index):
        carried_value = jnp.dot(hidden, adapter_input_weight[loop_index].T, preferred_element_type=jnp.float32)
        return total + jnp.where((storage == loop_index)[:, None], carried_value, jnp.float32(0.0)), None

    initial_inner = jnp.zeros((hidden.shape[0], adapter_input_weight.shape[1]), jnp.float32)
    low_rank_inner, unused_item = lax.scan(inner_update, initial_inner, jnp.arange(adapter_input_weight.shape[0], dtype=jnp.int32))
    low_rank_inner = low_rank_inner.astype(jnp.bfloat16)

    def delta_update(total, loop_index):
        carried_value = jnp.dot(low_rank_inner, adapter_output_weight[loop_index], preferred_element_type=jnp.float32)
        return total + jnp.where((storage == loop_index)[:, None], carried_value, jnp.float32(0.0)), None

    initial_delta = jnp.zeros((hidden.shape[0], adapter_output_weight.shape[2]), jnp.float32)
    adapter_delta, unused_item = lax.scan(delta_update, initial_delta, jnp.arange(adapter_output_weight.shape[0], dtype=jnp.int32))
    adapter_delta = lax.optimization_barrier(adapter_delta.astype(jnp.bfloat16))
    return (base + adapter_delta.astype(jnp.float32)).astype(jnp.bfloat16)
```

```python
import functools

import jax
import jax.numpy as jnp
from jax import lax
from jax.experimental import pallas as pl
from jax.experimental.pallas import tpu as pltpu
from jax.sharding import PartitionSpec as P

MESH = pl.DeviceIdType.MESH


def tile_of(extent, most):
    size = min(extent, most)
    while extent % size:
        size //= 2
    return size


def kernel(
    n_r,
    n_t,
    piece,
    rank,
    table_ref,
    row_ref,
    hidden_ref,
    w_ref,
    a_ref,
    b_ref,
    out_ref,
    gathered,
    base_in,
    w_v,
    a_v,
    b_v,
    acc,
    store_all,
    inner,
    inner_slots,
    part_send,
    part_slots,
    own_sem,
    ownb_sem,
    w_sem,
    ab_sem,
    g_send,
    g_recv,
    h_send,
    h_recv,
    st_send,
    st_recv,
    in_send,
    in_recv,
    p_send,
    p_recv,
):
    q = lax.axis_index("req")
    t = lax.axis_index("tensor")
    rows, units = hidden_ref.shape
    lanes, width = b_ref.shape
    resident = lanes // rank
    base_units, adapter_units = units // n_r, units // n_t
    c_base, c_adapter = base_units // piece, adapter_units // piece
    home = (q * base_units) // adapter_units
    first = (q * base_units) % adapter_units // piece if c_base != c_adapter else 0
    my_rows = pl.ds(pl.multiple_of(q * rows, rows), rows)

    def block(b):
        return pl.ds(pl.multiple_of(b * rows, rows), rows)

    def own_slice(c):
        return hidden_ref.at[:, pl.ds(pl.multiple_of(t * adapter_units + c * piece, 128), piece)]

    own = [
        pltpu.make_async_copy(own_slice(c), gathered.at[c, my_rows, :], own_sem.at[c])
        for c in range(c_adapter)
    ]
    own_base = [
        pltpu.make_async_copy(
            hidden_ref.at[:, pl.ds(pl.multiple_of(q * base_units + j * piece, 128), piece)],
            base_in.at[j, my_rows, :],
            ownb_sem.at[j],
        )
        for j in range(c_base)
    ]
    load_w = [
        pltpu.make_async_copy(
            w_ref.at[pl.ds(j * piece, piece), :], w_v.at[pl.ds(j * piece, piece), :], w_sem.at[j]
        )
        for j in range(c_base)
    ]
    load_a = pltpu.make_async_copy(a_ref, a_v, ab_sem.at[0])
    load_b = pltpu.make_async_copy(b_ref, b_v, ab_sem.at[1])

    barrier = pltpu.get_barrier_semaphore()

    @pl.loop(1, n_r)
    def _(i):
        pl.semaphore_signal(
            barrier, inc=1, device_id={"req": lax.rem(q + i, n_r)}, device_id_type=MESH
        )

    @pl.loop(1, n_t)
    def _(i):
        pl.semaphore_signal(
            barrier, inc=1, device_id={"tensor": lax.rem(t + i, n_t)}, device_id_type=MESH
        )

    own[0].start()
    own_base[0].start()
    load_a.start()
    for c in range(1, c_adapter):
        own[c].start()
    for j in range(c_base):
        if j:
            own_base[j].start()
        load_w[j].start()
    load_b.start()

    row_at = lax.broadcasted_iota(jnp.int32, (rows, lanes), 0)

    def put_row(r, held):
        return jnp.where(row_at == r, table_ref[row_ref[r]], held)

    store_all[my_rows, :] = lax.fori_loop(0, rows, put_row, jnp.zeros((rows, lanes), jnp.int32))
    acc[...] = jnp.zeros_like(acc)
    inner[...] = jnp.zeros_like(inner)
    pl.semaphore_wait(barrier, n_r + n_t - 2)

    def pass_on(b, c, to, side, from_own):
        return pltpu.make_async_remote_copy(
            src_ref=own_slice(c) if from_own else gathered.at[c, block(b), :],
            dst_ref=gathered.at[c, block(b), :],
            send_sem=g_send.at[side, b, c],
            recv_sem=g_recv.at[b, c],
            device_id={"req": to},
            device_id_type=MESH,
        )

    def send_own(c):
        @pl.when(q < n_r - 1)
        def _():
            pass_on(q, c, q + 1, 0, True).start()

        @pl.when(q > 0)
        def _():
            pass_on(q, c, q - 1, 1, True).start()

    def to_mate(b, c, j, i):
        return pltpu.make_async_remote_copy(
            src_ref=gathered.at[c, block(b), :],
            dst_ref=base_in.at[j, block(b), :],
            send_sem=h_send.at[i - 1, b, j],
            recv_sem=h_recv.at[b, j],
            device_id={"tensor": lax.rem(t + i, n_t)},
            device_id_type=MESH,
        )

    def to_self(b, c, j):
        return pltpu.make_async_copy(
            gathered.at[c, block(b), :], base_in.at[j, block(b), :], h_recv.at[b, j]
        )

    def store_copy(i):
        return pltpu.make_async_remote_copy(
            src_ref=store_all.at[my_rows, :],
            dst_ref=store_all.at[my_rows, :],
            send_sem=st_send.at[i],
            recv_sem=st_recv.at[q],
            device_id={"req": lax.rem(q + i, n_r)},
            device_id_type=MESH,
        )

    send_own(0)

    @pl.loop(1, n_r)
    def _(i):
        store_copy(i).start()

    send_own(1)

    row_tile = tile_of(n_r * rows, 128)
    col_tile = tile_of(width, 512)

    for c in range(c_adapter):
        in_base = (c >= first) & (c < first + c_base)
        j = c - first

        def arrived(b, forward, side):
            pass_on(b, c, 0, side, False).wait_recv()

            @pl.when((forward >= 0) & (forward < n_r))
            def _():
                pass_on(b, c, forward, side, False).start()

            @pl.when((t == home) & in_base)
            def _():
                for i in range(1, n_t):
                    to_mate(b, c, j, i).start()
                to_self(b, c, j).start()

        @pl.loop(1, n_r)
        def _(k):
            @pl.when(q - k >= 0)
            def _():
                arrived(q - k, q + 1, 0)

            @pl.when(q + k < n_r)
            def _():
                arrived(q + k, q - 1, 1)

        if c + 2 < c_adapter:
            send_own(c + 2)
        if c == 0:
            load_a.wait()
        own[c].wait()

        @pl.loop(0, n_r * rows // row_tile)
        def _(m):
            at = pl.ds(pl.multiple_of(m * row_tile, row_tile), row_tile)
            inner[at, :] += lax.dot_general(
                gathered[c, at, :],
                a_v[:, pl.ds(c * piece, piece)],
                (((1,), (1,)), ((), ())),
                preferred_element_type=jnp.float32,
            )

        @pl.when(in_base)
        def _():
            pltpu.make_async_copy(
                hidden_ref.at[:, pl.ds(0, piece)], base_in.at[j, my_rows, :], ownb_sem.at[j]
            ).wait()
            pltpu.make_async_copy(
                w_ref.at[pl.ds(0, piece), :], w_v.at[pl.ds(0, piece), :], w_sem.at[j]
            ).wait()

            @pl.loop(1, n_r)
            def _(i):
                to_self(lax.rem(q + i, n_r), c, j).wait()

            @pl.loop(0, n_r * rows // row_tile)
            def _(m):
                at = pl.ds(pl.multiple_of(m * row_tile, row_tile), row_tile)

                @pl.loop(0, width // col_tile)
                def _(n):
                    cols = pl.ds(pl.multiple_of(n * col_tile, col_tile), col_tile)
                    acc[at, cols] += jnp.dot(
                        base_in[j, at, :],
                        w_v[pl.ds(pl.multiple_of(j * piece, piece), piece), cols],
                        preferred_element_type=jnp.float32,
                    )

    @pl.loop(1, n_r)
    def _(i):
        pltpu.make_async_copy(
            store_all.at[my_rows, :],
            store_all.at[block(lax.rem(q + i, n_r)), :],
            st_recv.at[lax.rem(q + i, n_r)],
        ).wait()

    lane_adapter = lax.broadcasted_iota(jnp.int32, (n_r * rows, lanes), 1) // rank + q * resident
    inner[...] = jnp.where(store_all[...] == lane_adapter, inner[...], jnp.float32(0.0))

    def inner_copy(i):
        return pltpu.make_async_remote_copy(
            src_ref=inner,
            dst_ref=inner_slots.at[t],
            send_sem=in_send.at[i],
            recv_sem=in_recv.at[t],
            device_id={"tensor": lax.rem(t + i, n_t)},
            device_id_type=MESH,
        )

    def inner_arrival(i):
        mate = lax.rem(t + i, n_t)
        return pltpu.make_async_copy(inner, inner_slots.at[mate], in_recv.at[mate])

    @pl.loop(1, n_t)
    def _(i):
        inner_copy(i).start()

    load_b.wait()

    @pl.loop(1, n_t)
    def _(i):
        inner_arrival(i).wait()

    inner_slots[t] = inner[...]
    total = inner_slots[0]
    for s in range(1, n_t):
        total = total + inner_slots[s]

    def part_copy(d, i):
        return pltpu.make_async_remote_copy(
            src_ref=part_send.at[d],
            dst_ref=part_slots.at[q],
            send_sem=p_send.at[i],
            recv_sem=p_recv.at[q],
            device_id={"req": d},
            device_id_type=MESH,
        )

    inner_slots[0] = total

    def finish_block(d):
        low = inner_slots[0, block(d), :].astype(jnp.bfloat16)
        delta = jnp.dot(low, b_v[...], preferred_element_type=jnp.float32).astype(jnp.bfloat16)
        return acc[block(d), :] + delta.astype(jnp.float32)

    @pl.loop(1, n_r)
    def _(i):
        d = lax.rem(q + i, n_r)
        part_send[d] = finish_block(d).astype(jnp.bfloat16)
        part_copy(d, i).start()

    acc[my_rows, :] = finish_block(q)

    @pl.loop(1, n_r)
    def _(i):
        s = lax.rem(q + i, n_r)
        pltpu.make_async_copy(part_send.at[s], part_slots.at[s], p_recv.at[s]).wait()
        acc[my_rows, :] += part_slots[s].astype(jnp.float32)

    out_ref[...] = acc[my_rows, :].astype(jnp.bfloat16)

    @pl.loop(1, n_r)
    def _(i):
        part_copy(lax.rem(q + i, n_r), i).wait_send()
        store_copy(i).wait_send()

    @pl.loop(1, n_t)
    def _(i):
        inner_copy(i).wait_send()

    for c in range(c_adapter):
        in_base = (c >= first) & (c < first + c_base)
        j = c - first

        @pl.loop(0, n_r)
        def _(b):
            @pl.when((b <= q) & (q < n_r - 1))
            def _():
                pass_on(b, c, 0, 0, False).wait_send()

            @pl.when((b >= q) & (q > 0))
            def _():
                pass_on(b, c, 0, 1, False).wait_send()

            @pl.when((b != q) & (t == home) & in_base)
            def _():
                for i in range(1, n_t):
                    to_mate(b, c, j, i).wait_send()


def per_device(
    n_r,
    n_t,
    hidden,
    down_weight,
    adapter_input_weight,
    adapter_output_weight,
    adapter_storage_index,
    row_adapter_index,
):
    rows, units = hidden.shape
    resident, rank, adapter_units = adapter_input_weight.shape
    base_units, width = down_weight.shape
    lanes = resident * rank
    piece = min(base_units, adapter_units // 4)
    c_base, c_adapter = base_units // piece, adapter_units // piece
    everyone = n_r * rows
    hbm = pl.BlockSpec(memory_space=pl.ANY)
    smem = pl.BlockSpec(memory_space=pltpu.SMEM)
    bf16, f32 = jnp.bfloat16, jnp.float32
    dma = pltpu.SemaphoreType.DMA
    return pl.pallas_call(
        functools.partial(kernel, n_r, n_t, piece, rank),
        out_shape=jax.ShapeDtypeStruct((rows, width), bf16),
        in_specs=[smem, smem, hbm, hbm, hbm, hbm],
        out_specs=pl.BlockSpec(memory_space=pltpu.VMEM),
        scratch_shapes=[
            pltpu.VMEM((c_adapter, everyone, piece), bf16),
            pltpu.VMEM((c_base, everyone, piece), bf16),
            pltpu.VMEM((base_units, width), bf16),
            pltpu.VMEM((lanes, adapter_units), bf16),
            pltpu.VMEM((lanes, width), bf16),
            pltpu.VMEM((everyone, width), f32),
            pltpu.VMEM((everyone, lanes), jnp.int32),
            pltpu.VMEM((everyone, lanes), f32),
            pltpu.VMEM((n_t, everyone, lanes), f32),
            pltpu.VMEM((n_r, rows, width), bf16),
            pltpu.VMEM((n_r, rows, width), bf16),
            dma((c_adapter,)),
            dma((c_base,)),
            dma((c_base,)),
            dma((2,)),
            dma((2, n_r, c_adapter)),
            dma((n_r, c_adapter)),
            dma((n_t - 1, n_r, c_base)),
            dma((n_r, c_base)),
            dma((n_r,)),
            dma((n_r,)),
            dma((n_t,)),
            dma((n_t,)),
            dma((n_r,)),
            dma((n_r,)),
        ],
        compiler_params=pltpu.CompilerParams(
            collective_id=0, has_side_effects=True, vmem_limit_bytes=56 * 1024 * 1024
        ),
    )(
        adapter_storage_index,
        row_adapter_index,
        hidden,
        down_weight,
        adapter_input_weight.reshape(lanes, adapter_units),
        adapter_output_weight.reshape(lanes, width),
    )


def solution(mesh):
    in_specs = (
        P(("group", "req"), None),
        P("req", "tensor"),
        P("req", None, "tensor"),
        P("req", None, "tensor"),
        P("group"),
        P(("group", "req")),
    )
    out_specs = P(("group", "req"), "tensor")
    return jax.shard_map(
        functools.partial(per_device, mesh.shape["req"], mesh.shape["tensor"]),
        mesh=mesh,
        in_specs=in_specs,
        out_specs=out_specs,
        check_vma=False,
    )
```

```python
import functools

import jax
import jax.numpy as jnp
from jax import lax
from jax.experimental import pallas as pl
from jax.experimental.pallas import tpu as pltpu
from jax.sharding import PartitionSpec as P

MESH = pl.DeviceIdType.MESH


def tile_of(extent, most):
    size = min(extent, most)
    while extent % size:
        size //= 2
    return size


def kernel(
    n_r,
    n_t,
    piece,
    rank,
    table_ref,
    row_ref,
    hidden_ref,
    w_ref,
    a_ref,
    b_ref,
    out_ref,
    gathered,
    base_in,
    w_v,
    a_v,
    b_v,
    acc,
    store_all,
    inner,
    inner_slots,
    part_send,
    part_slots,
    a_help,
    help_out,
    help_in,
    own_sem,
    ownb_sem,
    w_sem,
    ab_sem,
    g_send,
    g_recv,
    h_send,
    h_recv,
    st_send,
    st_recv,
    in_send,
    in_recv,
    p_send,
    p_recv,
    ah_sem,
    help_send,
    help_recv,
):
    q = lax.axis_index("req")
    t = lax.axis_index("tensor")
    rows, units = hidden_ref.shape
    lanes, width = b_ref.shape
    resident = lanes // rank
    base_units, adapter_units = units // n_r, units // n_t
    c_base, c_adapter = base_units // piece, adapter_units // piece
    home = (q * base_units) // adapter_units
    first = (q * base_units) % adapter_units // piece if c_base != c_adapter else 0
    my_rows = pl.ds(pl.multiple_of(q * rows, rows), rows)

    def block(b):
        return pl.ds(pl.multiple_of(b * rows, rows), rows)

    def own_slice(c):
        return hidden_ref.at[:, pl.ds(pl.multiple_of(t * adapter_units + c * piece, 128), piece)]

    own = [
        pltpu.make_async_copy(own_slice(c), gathered.at[c, my_rows, :], own_sem.at[c])
        for c in range(c_adapter)
    ]
    own_base = [
        pltpu.make_async_copy(
            hidden_ref.at[:, pl.ds(pl.multiple_of(q * base_units + j * piece, 128), piece)],
            base_in.at[j, my_rows, :],
            ownb_sem.at[j],
        )
        for j in range(c_base)
    ]
    load_w = [
        pltpu.make_async_copy(
            w_ref.at[pl.ds(j * piece, piece), :], w_v.at[pl.ds(j * piece, piece), :], w_sem.at[j]
        )
        for j in range(c_base)
    ]
    load_a = pltpu.make_async_copy(a_ref, a_v, ab_sem.at[0])
    load_b = pltpu.make_async_copy(b_ref, b_v, ab_sem.at[1])

    barrier = pltpu.get_barrier_semaphore()

    @pl.loop(1, n_r)
    def _(i):
        pl.semaphore_signal(
            barrier, inc=1, device_id={"req": lax.rem(q + i, n_r)}, device_id_type=MESH
        )

    @pl.loop(1, n_t)
    def _(i):
        pl.semaphore_signal(
            barrier, inc=1, device_id={"tensor": lax.rem(t + i, n_t)}, device_id_type=MESH
        )

    own[0].start()
    own_base[0].start()
    load_a.start()
    for c in range(1, c_adapter):
        own[c].start()
    for j in range(c_base):
        if j:
            own_base[j].start()
        load_w[j].start()
    load_b.start()

    row_at = lax.broadcasted_iota(jnp.int32, (rows, lanes), 0)

    def put_row(r, held):
        return jnp.where(row_at == r, table_ref[row_ref[r]], held)

    store_all[my_rows, :] = lax.fori_loop(0, rows, put_row, jnp.zeros((rows, lanes), jnp.int32))
    acc[...] = jnp.zeros_like(acc)
    pl.semaphore_wait(barrier, n_r + n_t - 2)

    lent_from = c_adapter // 2 if n_r >= 4 else c_adapter
    last_home = ((n_r - 1) * base_units) // adapter_units
    lends_low = lax.rem(t, 2) == 1
    lends_high = lax.rem(t + last_home, 2) == 1

    def lent(to):
        return ((to == 0) & lends_low) | ((to == n_r - 1) & lends_high)

    def travels(c, to):
        return jnp.logical_not(lent(to)) if c >= lent_from else to >= 0

    lends = lent(q)
    helps = ((q == 1) & lends_low) | ((q == n_r - 2) & lends_high)
    lent_columns = pl.ds(lent_from * piece, (c_adapter - lent_from) * piece)

    def lend_copy():
        return pltpu.make_async_remote_copy(
            src_ref=a_ref.at[:, lent_columns],
            dst_ref=a_help,
            send_sem=ah_sem.at[0],
            recv_sem=ah_sem.at[1],
            device_id={"req": jnp.where(q == 0, 1, n_r - 2)},
            device_id_type=MESH,
        )

    def help_copy(b):
        return pltpu.make_async_remote_copy(
            src_ref=help_out.at[block(b), :],
            dst_ref=help_in.at[block(b), :],
            send_sem=help_send.at[b],
            recv_sem=help_recv.at[b],
            device_id={"req": jnp.where(q == 1, 0, n_r - 1)},
            device_id_type=MESH,
        )

    def pass_on(b, c, to, side, from_own):
        return pltpu.make_async_remote_copy(
            src_ref=own_slice(c) if from_own else gathered.at[c, block(b), :],
            dst_ref=gathered.at[c, block(b), :],
            send_sem=g_send.at[side, b, c],
            recv_sem=g_recv.at[b, c],
            device_id={"req": to},
            device_id_type=MESH,
        )

    def send_own(c):
        @pl.when((q < n_r - 1) & travels(c, q + 1))
        def _():
            pass_on(q, c, q + 1, 0, True).start()

        @pl.when((q > 0) & travels(c, q - 1))
        def _():
            pass_on(q, c, q - 1, 1, True).start()

    paired = t + 1 - 2 * lax.rem(t, 2)
    relays = (lax.rem(t, 2) == lax.rem(home, 2)) & (t != home)

    def to_mate(b, c, j, i, relayed):
        to = paired if i == 0 else lax.rem(t + 2 * i, n_t)
        return pltpu.make_async_remote_copy(
            src_ref=base_in.at[j, block(b), :] if relayed else gathered.at[c, block(b), :],
            dst_ref=base_in.at[j, block(b), :],
            send_sem=h_send.at[i, b, j],
            recv_sem=h_recv.at[b, j],
            device_id={"tensor": to},
            device_id_type=MESH,
        )

    def to_self(b, c, j):
        return pltpu.make_async_copy(
            gathered.at[c, block(b), :], base_in.at[j, block(b), :], h_recv.at[b, j]
        )

    def store_copy(i):
        return pltpu.make_async_remote_copy(
            src_ref=store_all.at[my_rows, :],
            dst_ref=store_all.at[my_rows, :],
            send_sem=st_send.at[i],
            recv_sem=st_recv.at[q],
            device_id={"req": lax.rem(q + i, n_r)},
            device_id_type=MESH,
        )

    def inner_copy(b, i):
        return pltpu.make_async_remote_copy(
            src_ref=inner.at[block(b), :],
            dst_ref=inner_slots.at[t, block(b), :],
            send_sem=in_send.at[i, b],
            recv_sem=in_recv.at[t, b],
            device_id={"tensor": lax.rem(t + i, n_t)},
            device_id_type=MESH,
        )

    def part_copy(d):
        return pltpu.make_async_remote_copy(
            src_ref=part_send.at[d],
            dst_ref=part_slots.at[q],
            send_sem=p_send.at[d],
            recv_sem=p_recv.at[q],
            device_id={"req": d},
            device_id_type=MESH,
        )

    for c in range(c_adapter):
        send_own(c)
        if c == 0:

            @pl.loop(1, n_r)
            def _(i):
                store_copy(i).start()

            if lent_from < c_adapter:

                @pl.when(lends)
                def _():
                    lend_copy().start()

    col_tile = tile_of(width, 1024)

    def base_chunk(c):
        return (c >= first) & (c < first + c_base), c - first

    def arrive(b, c, forward, side):
        in_base, j = base_chunk(c)

        @pl.when(travels(c, q))
        def _():
            pass_on(b, c, 0, side, False).wait_recv()

        @pl.when((forward >= 0) & (forward < n_r) & travels(c, forward))
        def _():
            pass_on(b, c, forward, side, False).start()

        @pl.when((t == home) & in_base)
        def _():
            for i in reversed(range(n_t // 2)):
                to_mate(b, c, j, i, False).start()
            to_self(b, c, j).start()

    def rank_product(b, c):
        at = block(b)

        @pl.when(travels(c, q) | (b == q))
        def _():
            product = lax.dot_general(
                gathered[c, at, :],
                a_v[:, pl.ds(c * piece, piece)],
                (((1,), (1,)), ((), ())),
                preferred_element_type=jnp.float32,
            )
            if c == 0:
                inner[at, :] = product
            else:
                inner[at, :] += product

    def base_product(at, c):
        in_base, j = base_chunk(c)

        @pl.when(in_base)
        def _():
            @pl.loop(0, width // col_tile)
            def _(n):
                cols = pl.ds(pl.multiple_of(n * col_tile, col_tile), col_tile)
                acc[at, cols] += jnp.dot(
                    base_in[j, at, :],
                    w_v[pl.ds(pl.multiple_of(j * piece, piece), piece), cols],
                    preferred_element_type=jnp.float32,
                )

    def ready(b, c):
        in_base, j = base_chunk(c)

        @pl.when(in_base)
        def _():
            to_self(b, c, j).wait()

            @pl.when(relays)
            def _():
                to_mate(b, c, j, 0, True).start()

    def multiply(b, c):
        ready(b, c)
        rank_product(b, c)
        base_product(block(b), c)

    def multiply_near(c):
        own[c].wait()
        both(1, lambda b, to, side: ready(b, c))
        rank_product(q, c)
        both(1, lambda b, to, side: rank_product(b, c))
        in_base, j = base_chunk(c)

        @pl.when(in_base)
        def _():
            pltpu.make_async_copy(
                hidden_ref.at[:, pl.ds(0, piece)], base_in.at[j, my_rows, :], ownb_sem.at[j]
            ).wait()
            pltpu.make_async_copy(
                w_ref.at[pl.ds(0, piece), :], w_v.at[pl.ds(0, piece), :], w_sem.at[j]
            ).wait()

        at_end = (q == 0) | (q == n_r - 1)
        start = pl.multiple_of(jnp.maximum(q - 1, 0) * rows, rows)

        @pl.when(at_end)
        def _():
            base_product(pl.ds(start, 2 * rows), c)

        if n_r > 2:

            @pl.when(jnp.logical_not(at_end))
            def _():
                base_product(pl.ds(start, 3 * rows), c)

    def assist(b):
        at = block(b)
        help_out[at, :] = sum(
            lax.dot_general(
                gathered[c, at, :],
                a_help[:, pl.ds((c - lent_from) * piece, piece)],
                (((1,), (1,)), ((), ())),
                preferred_element_type=jnp.float32,
            )
            for c in range(lent_from, c_adapter)
        )
        help_copy(b).start()

    def assist_from(b, to, side):
        @pl.when(helps & jnp.where(side == 0, q == n_r - 2, q == 1))
        def _():
            assist(b)

    def exchange(b, mine):
        at = block(b)
        if not mine:
            pltpu.make_async_copy(store_all.at[my_rows, :], store_all.at[at, :], st_recv.at[b]).wait()

            @pl.when(lends)
            def _():
                pltpu.make_async_copy(
                    help_out.at[at, :], help_in.at[at, :], help_recv.at[b]
                ).wait()
                inner[at, :] += help_in[at, :]

        lane_adapter = lax.broadcasted_iota(jnp.int32, (rows, lanes), 1) // rank + q * resident
        inner[at, :] = jnp.where(store_all[at, :] == lane_adapter, inner[at, :], jnp.float32(0.0))

        @pl.loop(1, n_t)
        def _(i):
            inner_copy(b, i).start()

    def finish(b):
        at = block(b)

        @pl.loop(1, n_t)
        def _(i):
            mate = lax.rem(t + i, n_t)
            pltpu.make_async_copy(
                inner.at[at, :], inner_slots.at[mate, at, :], in_recv.at[mate, b]
            ).wait()

        inner_slots[t, at, :] = inner[at, :]
        total = inner_slots[0, at, :]
        for s in range(1, n_t):
            total = total + inner_slots[s, at, :]
        delta = jnp.dot(
            total.astype(jnp.bfloat16), b_v[...], preferred_element_type=jnp.float32
        ).astype(jnp.bfloat16)
        return acc[at, :] + delta.astype(jnp.float32)

    def both(k, act):
        @pl.when((q - k >= 0) & (k > 0))
        def _():
            act(q - k, q + 1, 0)

        @pl.when((q + k < n_r) & (k > 0))
        def _():
            act(q + k, q - 1, 1)

    def hand_back(b, *_):
        part_send[b] = finish(b).astype(jnp.bfloat16)
        part_copy(b).start()

    last = c_adapter - 1
    load_a.wait()

    @pl.loop(1, n_r)
    def _(k):
        for c in range(c_adapter):
            both(k, lambda b, to, side: arrive(b, c, to, side))

            if c:

                @pl.when(k == 1)
                def _():
                    multiply_near(c - 1)

                @pl.when(k > 1)
                def _():
                    both(k, lambda b, to, side: multiply(b, c - 1))
            else:

                @pl.when(k == 2)
                def _():
                    multiply_near(last)
                    exchange(q, True)
                    load_b.wait()

                @pl.when(k > 2)
                def _():
                    both(k - 1, lambda b, to, side: multiply(b, last))
            if c == min(1, last) and lent_from < c_adapter:

                @pl.when((k == 2) & helps)
                def _():
                    lend_copy().wait_recv()
                    assist(q)

                both(k - 1, assist_from)
            if c == min(2, last):
                both(k - 2, hand_back)
            if c == last:
                both(k - 1, lambda b, to, side: exchange(b, False))

    both(n_r - 1, lambda b, to, side: multiply(b, last))
    both(n_r - 1, lambda b, to, side: exchange(b, False))
    both(n_r - 2, hand_back)
    acc[my_rows, :] = finish(q)
    both(n_r - 1, hand_back)

    @pl.loop(1, n_r)
    def _(i):
        s = lax.rem(q + i, n_r)
        pltpu.make_async_copy(part_send.at[s], part_slots.at[s], p_recv.at[s]).wait()
        acc[my_rows, :] += part_slots[s].astype(jnp.float32)

    out_ref[...] = acc[my_rows, :].astype(jnp.bfloat16)

    if lent_from < c_adapter:

        @pl.when(lends)
        def _():
            lend_copy().wait_send()

        @pl.loop(0, n_r)
        def _(b):
            @pl.when(helps & jnp.where(q == 1, b > 0, b < n_r - 1))
            def _():
                help_copy(b).wait_send()

    @pl.loop(1, n_r)
    def _(i):
        part_copy(lax.rem(q + i, n_r)).wait_send()
        store_copy(i).wait_send()

    @pl.loop(0, n_r)
    def _(b):
        @pl.loop(1, n_t)
        def _(i):
            inner_copy(b, i).wait_send()

        for c in range(c_adapter):
            in_base, j = base_chunk(c)

            @pl.when((b <= q) & (q < n_r - 1) & travels(c, q + 1))
            def _():
                pass_on(b, c, 0, 0, False).wait_send()

            @pl.when((b >= q) & (q > 0) & travels(c, q - 1))
            def _():
                pass_on(b, c, 0, 1, False).wait_send()

            @pl.when((b != q) & (t == home) & in_base)
            def _():
                for i in range(n_t // 2):
                    to_mate(b, c, j, i, False).wait_send()

            @pl.when((b != q) & relays & in_base)
            def _():
                to_mate(b, c, j, 0, True).wait_send()


def per_device(
    n_r,
    n_t,
    hidden,
    down_weight,
    adapter_input_weight,
    adapter_output_weight,
    adapter_storage_index,
    row_adapter_index,
):
    rows, units = hidden.shape
    resident, rank, adapter_units = adapter_input_weight.shape
    base_units, width = down_weight.shape
    lanes = resident * rank
    piece = min(base_units, adapter_units // 4)
    c_base, c_adapter = base_units // piece, adapter_units // piece
    everyone = n_r * rows
    hbm = pl.BlockSpec(memory_space=pl.ANY)
    smem = pl.BlockSpec(memory_space=pltpu.SMEM)
    bf16, f32 = jnp.bfloat16, jnp.float32
    dma = pltpu.SemaphoreType.DMA
    return pl.pallas_call(
        functools.partial(kernel, n_r, n_t, piece, rank),
        out_shape=jax.ShapeDtypeStruct((rows, width), bf16),
        in_specs=[smem, smem, hbm, hbm, hbm, hbm],
        out_specs=pl.BlockSpec(memory_space=pltpu.VMEM),
        scratch_shapes=[
            pltpu.VMEM((c_adapter, everyone, piece), bf16),
            pltpu.VMEM((c_base, everyone, piece), bf16),
            pltpu.VMEM((base_units, width), bf16),
            pltpu.VMEM((lanes, adapter_units), bf16),
            pltpu.VMEM((lanes, width), bf16),
            pltpu.VMEM((everyone, width), f32),
            pltpu.VMEM((everyone, lanes), jnp.int32),
            pltpu.VMEM((everyone, lanes), f32),
            pltpu.VMEM((n_t, everyone, lanes), f32),
            pltpu.VMEM((n_r, rows, width), bf16),
            pltpu.VMEM((n_r, rows, width), bf16),
            pltpu.VMEM((lanes, piece * c_adapter // 2), bf16),
            pltpu.VMEM((everyone, lanes), f32),
            pltpu.VMEM((everyone, lanes), f32),
            dma((c_adapter,)),
            dma((c_base,)),
            dma((c_base,)),
            dma((2,)),
            dma((2, n_r, c_adapter)),
            dma((n_r, c_adapter)),
            dma((n_t // 2, n_r, c_base)),
            dma((n_r, c_base)),
            dma((n_r,)),
            dma((n_r,)),
            dma((n_t, n_r)),
            dma((n_t, n_r)),
            dma((n_r,)),
            dma((n_r,)),
            dma((2,)),
            dma((n_r,)),
            dma((n_r,)),
        ],
        compiler_params=pltpu.CompilerParams(
            collective_id=0, has_side_effects=True, vmem_limit_bytes=56 * 1024 * 1024
        ),
    )(
        adapter_storage_index,
        row_adapter_index,
        hidden,
        down_weight,
        adapter_input_weight.reshape(lanes, adapter_units),
        adapter_output_weight.reshape(lanes, width),
    )


def solution(mesh):
    in_specs = (
        P(("group", "req"), None),
        P("req", "tensor"),
        P("req", None, "tensor"),
        P("req", None, "tensor"),
        P("group"),
        P(("group", "req")),
    )
    out_specs = P(("group", "req"), "tensor")
    return jax.shard_map(
        functools.partial(per_device, mesh.shape["req"], mesh.shape["tensor"]),
        mesh=mesh,
        in_specs=in_specs,
        out_specs=out_specs,
        check_vma=False,
    )
```

```python
import functools

import jax
import jax.numpy as jnp
from jax import lax
from jax.experimental import pallas as pl
from jax.experimental.pallas import tpu as pltpu
from jax.sharding import PartitionSpec as P

MESH = pl.DeviceIdType.MESH


def tile_of(extent, most):
    size = min(extent, most)
    while extent % size:
        size //= 2
    return size


def kernel(
    n_r,
    n_t,
    piece,
    rank,
    table_ref,
    row_ref,
    hidden_ref,
    w_ref,
    a_ref,
    b_ref,
    out_ref,
    gathered,
    base_in,
    w_v,
    a_v,
    b_v,
    acc,
    store_all,
    inner,
    inner_slots,
    part_send,
    part_slots,
    a_help,
    help_out,
    help_in,
    own_sem,
    ownb_sem,
    w_sem,
    ab_sem,
    g_send,
    g_recv,
    h_send,
    h_recv,
    st_send,
    st_recv,
    in_send,
    in_recv,
    p_send,
    p_recv,
    ah_sem,
    help_send,
    help_recv,
):
    q = lax.axis_index("req")
    t = lax.axis_index("tensor")
    rows, units = hidden_ref.shape
    lanes, width = b_ref.shape
    resident = lanes // rank
    base_units, adapter_units = units // n_r, units // n_t
    c_base, c_adapter = base_units // piece, adapter_units // piece
    home = (q * base_units) // adapter_units
    first = (q * base_units) % adapter_units // piece if c_base != c_adapter else 0
    my_rows = pl.ds(pl.multiple_of(q * rows, rows), rows)

    def block(b):
        return pl.ds(pl.multiple_of(b * rows, rows), rows)

    def own_slice(c):
        return hidden_ref.at[:, pl.ds(pl.multiple_of(t * adapter_units + c * piece, 128), piece)]

    own = [
        pltpu.make_async_copy(own_slice(c), gathered.at[c, my_rows, :], own_sem.at[c])
        for c in range(c_adapter)
    ]
    own_base = [
        pltpu.make_async_copy(
            hidden_ref.at[:, pl.ds(pl.multiple_of(q * base_units + j * piece, 128), piece)],
            base_in.at[j, my_rows, :],
            ownb_sem.at[j],
        )
        for j in range(c_base)
    ]
    load_w = [
        pltpu.make_async_copy(
            w_ref.at[pl.ds(j * piece, piece), :], w_v.at[pl.ds(j * piece, piece), :], w_sem.at[j]
        )
        for j in range(c_base)
    ]
    load_a = pltpu.make_async_copy(a_ref, a_v, ab_sem.at[0])
    load_b = pltpu.make_async_copy(b_ref, b_v, ab_sem.at[1])

    barrier = pltpu.get_barrier_semaphore()

    @pl.loop(1, n_r)
    def _(i):
        pl.semaphore_signal(
            barrier, inc=1, device_id={"req": lax.rem(q + i, n_r)}, device_id_type=MESH
        )

    @pl.loop(1, n_t)
    def _(i):
        pl.semaphore_signal(
            barrier, inc=1, device_id={"tensor": lax.rem(t + i, n_t)}, device_id_type=MESH
        )

    own[0].start()
    own_base[0].start()
    load_a.start()
    for c in range(1, c_adapter):
        own[c].start()
    for j in range(c_base):
        if j:
            own_base[j].start()
        load_w[j].start()
    load_b.start()

    row_at = lax.broadcasted_iota(jnp.int32, (rows, lanes), 0)

    def put_row(r, held):
        return jnp.where(row_at == r, table_ref[row_ref[r]], held)

    store_all[my_rows, :] = lax.fori_loop(0, rows, put_row, jnp.zeros((rows, lanes), jnp.int32))
    acc[...] = jnp.zeros_like(acc)
    pl.semaphore_wait(barrier, n_r + n_t - 2)

    lent_from = c_adapter // 2 if n_r >= 4 else c_adapter
    last_home = ((n_r - 1) * base_units) // adapter_units
    lends_low = lax.rem(t, 2) == 1
    lends_high = lax.rem(t + last_home, 2) == 1

    def lent(to):
        return ((to == 0) & lends_low) | ((to == n_r - 1) & lends_high)

    def travels(c, to):
        return jnp.logical_not(lent(to)) if c >= lent_from else to >= 0

    lends = lent(q)
    helps = ((q == 1) & lends_low) | ((q == n_r - 2) & lends_high)
    lent_columns = pl.ds(lent_from * piece, (c_adapter - lent_from) * piece)

    def lend_copy():
        return pltpu.make_async_remote_copy(
            src_ref=a_ref.at[:, lent_columns],
            dst_ref=a_help,
            send_sem=ah_sem.at[0],
            recv_sem=ah_sem.at[1],
            device_id={"req": jnp.where(q == 0, 1, n_r - 2)},
            device_id_type=MESH,
        )

    def help_copy(b):
        return pltpu.make_async_remote_copy(
            src_ref=help_out.at[block(b), :],
            dst_ref=help_in.at[block(b), :],
            send_sem=help_send.at[b],
            recv_sem=help_recv.at[b],
            device_id={"req": jnp.where(q == 1, 0, n_r - 1)},
            device_id_type=MESH,
        )

    def pass_on(b, c, to, side, from_own):
        return pltpu.make_async_remote_copy(
            src_ref=own_slice(c) if from_own else gathered.at[c, block(b), :],
            dst_ref=gathered.at[c, block(b), :],
            send_sem=g_send.at[side, b, c],
            recv_sem=g_recv.at[b, c],
            device_id={"req": to},
            device_id_type=MESH,
        )

    def send_own(c):
        @pl.when((q < n_r - 1) & travels(c, q + 1))
        def _():
            pass_on(q, c, q + 1, 0, False).start()

        @pl.when((q > 0) & travels(c, q - 1))
        def _():
            pass_on(q, c, q - 1, 1, False).start()

    paired = t + 1 - 2 * lax.rem(t, 2)
    relays = (lax.rem(t, 2) == lax.rem(home, 2)) & (t != home)

    def to_mate(b, c, j, i, relayed):
        to = paired if i == 0 else lax.rem(t + 2 * i, n_t)
        return pltpu.make_async_remote_copy(
            src_ref=base_in.at[j, block(b), :] if relayed else gathered.at[c, block(b), :],
            dst_ref=base_in.at[j, block(b), :],
            send_sem=h_send.at[i, b, j],
            recv_sem=h_recv.at[b, j],
            device_id={"tensor": to},
            device_id_type=MESH,
        )

    def to_self(b, c, j):
        return pltpu.make_async_copy(
            gathered.at[c, block(b), :], base_in.at[j, block(b), :], h_recv.at[b, j]
        )

    def store_copy(i):
        return pltpu.make_async_remote_copy(
            src_ref=store_all.at[my_rows, :],
            dst_ref=store_all.at[my_rows, :],
            send_sem=st_send.at[i],
            recv_sem=st_recv.at[q],
            device_id={"req": lax.rem(q + i, n_r)},
            device_id_type=MESH,
        )

    def inner_copy(b, i):
        return pltpu.make_async_remote_copy(
            src_ref=inner.at[block(b), :],
            dst_ref=inner_slots.at[t, block(b), :],
            send_sem=in_send.at[i, b],
            recv_sem=in_recv.at[t, b],
            device_id={"tensor": lax.rem(t + i, n_t)},
            device_id_type=MESH,
        )

    def part_copy(d):
        return pltpu.make_async_remote_copy(
            src_ref=part_send.at[d],
            dst_ref=part_slots.at[q],
            send_sem=p_send.at[d],
            recv_sem=p_recv.at[q],
            device_id={"req": d},
            device_id_type=MESH,
        )

    for c in range(c_adapter):
        own[c].wait()
        send_own(c)
        if c == 0:

            @pl.loop(1, n_r)
            def _(i):
                store_copy(i).start()

            if lent_from < c_adapter:

                @pl.when(lends)
                def _():
                    lend_copy().start()

    col_tile = tile_of(width, 1024)

    def base_chunk(c):
        return (c >= first) & (c < first + c_base), c - first

    def arrive(b, c, forward, side):
        in_base, j = base_chunk(c)

        @pl.when(travels(c, q))
        def _():
            pass_on(b, c, 0, side, False).wait_recv()

        @pl.when((forward >= 0) & (forward < n_r) & travels(c, forward))
        def _():
            pass_on(b, c, forward, side, False).start()

        @pl.when((t == home) & in_base)
        def _():
            for i in reversed(range(n_t // 2)):
                to_mate(b, c, j, i, False).start()
            to_self(b, c, j).start()

    def rank_product(b, c):
        at = block(b)

        @pl.when(travels(c, q) | (b == q))
        def _():
            product = lax.dot_general(
                gathered[c, at, :],
                a_v[:, pl.ds(c * piece, piece)],
                (((1,), (1,)), ((), ())),
                preferred_element_type=jnp.float32,
            )
            if c == 0:
                inner[at, :] = product
            else:
                inner[at, :] += product

    def base_product(at, c):
        in_base, j = base_chunk(c)

        @pl.when(in_base)
        def _():
            @pl.loop(0, width // col_tile)
            def _(n):
                cols = pl.ds(pl.multiple_of(n * col_tile, col_tile), col_tile)
                acc[at, cols] += jnp.dot(
                    base_in[j, at, :],
                    w_v[pl.ds(pl.multiple_of(j * piece, piece), piece), cols],
                    preferred_element_type=jnp.float32,
                )

    def ready(b, c):
        in_base, j = base_chunk(c)

        @pl.when(in_base)
        def _():
            to_self(b, c, j).wait()

            @pl.when(relays)
            def _():
                to_mate(b, c, j, 0, True).start()

    def multiply(b, c):
        ready(b, c)
        rank_product(b, c)
        base_product(block(b), c)

    def multiply_near(c):
        both(1, lambda b, to, side: ready(b, c))
        rank_product(q, c)
        both(1, lambda b, to, side: rank_product(b, c))
        in_base, j = base_chunk(c)

        @pl.when(in_base)
        def _():
            pltpu.make_async_copy(
                hidden_ref.at[:, pl.ds(0, piece)], base_in.at[j, my_rows, :], ownb_sem.at[j]
            ).wait()
            pltpu.make_async_copy(
                w_ref.at[pl.ds(0, piece), :], w_v.at[pl.ds(0, piece), :], w_sem.at[j]
            ).wait()

        at_end = (q == 0) | (q == n_r - 1)
        start = pl.multiple_of(jnp.maximum(q - 1, 0) * rows, rows)

        @pl.when(at_end)
        def _():
            base_product(pl.ds(start, 2 * rows), c)

        if n_r > 2:

            @pl.when(jnp.logical_not(at_end))
            def _():
                base_product(pl.ds(start, 3 * rows), c)

    def assist(b):
        at = block(b)
        help_out[at, :] = sum(
            lax.dot_general(
                gathered[c, at, :],
                a_help[:, pl.ds((c - lent_from) * piece, piece)],
                (((1,), (1,)), ((), ())),
                preferred_element_type=jnp.float32,
            )
            for c in range(lent_from, c_adapter)
        )
        help_copy(b).start()

    def assist_from(b, to, side):
        @pl.when(helps & jnp.where(side == 0, q == n_r - 2, q == 1))
        def _():
            assist(b)

    def exchange(b, mine):
        at = block(b)
        if not mine:
            pltpu.make_async_copy(store_all.at[my_rows, :], store_all.at[at, :], st_recv.at[b]).wait()

            @pl.when(lends)
            def _():
                pltpu.make_async_copy(
                    help_out.at[at, :], help_in.at[at, :], help_recv.at[b]
                ).wait()
                inner[at, :] += help_in[at, :]

        lane_adapter = lax.broadcasted_iota(jnp.int32, (rows, lanes), 1) // rank + q * resident
        inner[at, :] = jnp.where(store_all[at, :] == lane_adapter, inner[at, :], jnp.float32(0.0))

        @pl.loop(1, n_t)
        def _(i):
            inner_copy(b, i).start()

    def finish(b):
        at = block(b)

        @pl.loop(1, n_t)
        def _(i):
            mate = lax.rem(t + i, n_t)
            pltpu.make_async_copy(
                inner.at[at, :], inner_slots.at[mate, at, :], in_recv.at[mate, b]
            ).wait()

        inner_slots[t, at, :] = inner[at, :]
        total = inner_slots[0, at, :]
        for s in range(1, n_t):
            total = total + inner_slots[s, at, :]
        delta = jnp.dot(
            total.astype(jnp.bfloat16), b_v[...], preferred_element_type=jnp.float32
        ).astype(jnp.bfloat16)
        return acc[at, :] + delta.astype(jnp.float32)

    def both(k, act):
        @pl.when((q - k >= 0) & (k > 0))
        def _():
            act(q - k, q + 1, 0)

        @pl.when((q + k < n_r) & (k > 0))
        def _():
            act(q + k, q - 1, 1)

    def hand_back(b, *_):
        part_send[b] = finish(b).astype(jnp.bfloat16)
        part_copy(b).start()

    last = c_adapter - 1
    load_a.wait()

    @pl.loop(1, n_r)
    def _(k):
        for c in range(c_adapter):
            both(k, lambda b, to, side: arrive(b, c, to, side))

            if c:

                @pl.when(k == 1)
                def _():
                    multiply_near(c - 1)

                @pl.when(k > 1)
                def _():
                    both(k, lambda b, to, side: multiply(b, c - 1))
            else:

                @pl.when(k == 2)
                def _():
                    multiply_near(last)
                    exchange(q, True)
                    load_b.wait()

                @pl.when(k > 2)
                def _():
                    both(k - 1, lambda b, to, side: multiply(b, last))
            if c == min(1, last) and lent_from < c_adapter:

                @pl.when((k == 2) & helps)
                def _():
                    lend_copy().wait_recv()
                    assist(q)

                both(k - 1, assist_from)
            if c == min(2, last):
                both(k - 2, hand_back)
            if c == last:
                both(k - 1, lambda b, to, side: exchange(b, False))

    both(n_r - 1, lambda b, to, side: multiply(b, last))
    both(n_r - 1, lambda b, to, side: exchange(b, False))
    both(n_r - 2, hand_back)
    acc[my_rows, :] = finish(q)
    both(n_r - 1, hand_back)

    @pl.loop(1, n_r)
    def _(i):
        s = lax.rem(q + i, n_r)
        pltpu.make_async_copy(part_send.at[s], part_slots.at[s], p_recv.at[s]).wait()
        acc[my_rows, :] += part_slots[s].astype(jnp.float32)

    out_ref[...] = acc[my_rows, :].astype(jnp.bfloat16)

    if lent_from < c_adapter:

        @pl.when(lends)
        def _():
            lend_copy().wait_send()

        @pl.loop(0, n_r)
        def _(b):
            @pl.when(helps & jnp.where(q == 1, b > 0, b < n_r - 1))
            def _():
                help_copy(b).wait_send()

    @pl.loop(1, n_r)
    def _(i):
        part_copy(lax.rem(q + i, n_r)).wait_send()
        store_copy(i).wait_send()

    @pl.loop(0, n_r)
    def _(b):
        @pl.loop(1, n_t)
        def _(i):
            inner_copy(b, i).wait_send()

        for c in range(c_adapter):
            in_base, j = base_chunk(c)

            @pl.when((b <= q) & (q < n_r - 1) & travels(c, q + 1))
            def _():
                pass_on(b, c, 0, 0, False).wait_send()

            @pl.when((b >= q) & (q > 0) & travels(c, q - 1))
            def _():
                pass_on(b, c, 0, 1, False).wait_send()

            @pl.when((b != q) & (t == home) & in_base)
            def _():
                for i in range(n_t // 2):
                    to_mate(b, c, j, i, False).wait_send()

            @pl.when((b != q) & relays & in_base)
            def _():
                to_mate(b, c, j, 0, True).wait_send()


def per_device(
    n_r,
    n_t,
    hidden,
    down_weight,
    adapter_input_weight,
    adapter_output_weight,
    adapter_storage_index,
    row_adapter_index,
):
    rows, units = hidden.shape
    resident, rank, adapter_units = adapter_input_weight.shape
    base_units, width = down_weight.shape
    lanes = resident * rank
    piece = min(base_units, adapter_units // 4)
    c_base, c_adapter = base_units // piece, adapter_units // piece
    everyone = n_r * rows
    hbm = pl.BlockSpec(memory_space=pl.ANY)
    smem = pl.BlockSpec(memory_space=pltpu.SMEM)
    bf16, f32 = jnp.bfloat16, jnp.float32
    dma = pltpu.SemaphoreType.DMA
    return pl.pallas_call(
        functools.partial(kernel, n_r, n_t, piece, rank),
        out_shape=jax.ShapeDtypeStruct((rows, width), bf16),
        in_specs=[smem, smem, hbm, hbm, hbm, hbm],
        out_specs=pl.BlockSpec(memory_space=pltpu.VMEM),
        scratch_shapes=[
            pltpu.VMEM((c_adapter, everyone, piece), bf16),
            pltpu.VMEM((c_base, everyone, piece), bf16),
            pltpu.VMEM((base_units, width), bf16),
            pltpu.VMEM((lanes, adapter_units), bf16),
            pltpu.VMEM((lanes, width), bf16),
            pltpu.VMEM((everyone, width), f32),
            pltpu.VMEM((everyone, lanes), jnp.int32),
            pltpu.VMEM((everyone, lanes), f32),
            pltpu.VMEM((n_t, everyone, lanes), f32),
            pltpu.VMEM((n_r, rows, width), bf16),
            pltpu.VMEM((n_r, rows, width), bf16),
            pltpu.VMEM((lanes, piece * c_adapter // 2), bf16),
            pltpu.VMEM((everyone, lanes), f32),
            pltpu.VMEM((everyone, lanes), f32),
            dma((c_adapter,)),
            dma((c_base,)),
            dma((c_base,)),
            dma((2,)),
            dma((2, n_r, c_adapter)),
            dma((n_r, c_adapter)),
            dma((n_t // 2, n_r, c_base)),
            dma((n_r, c_base)),
            dma((n_r,)),
            dma((n_r,)),
            dma((n_t, n_r)),
            dma((n_t, n_r)),
            dma((n_r,)),
            dma((n_r,)),
            dma((2,)),
            dma((n_r,)),
            dma((n_r,)),
        ],
        compiler_params=pltpu.CompilerParams(
            collective_id=0, has_side_effects=True, vmem_limit_bytes=56 * 1024 * 1024
        ),
    )(
        adapter_storage_index,
        row_adapter_index,
        hidden,
        down_weight,
        adapter_input_weight.reshape(lanes, adapter_units),
        adapter_output_weight.reshape(lanes, width),
    )


def solution(mesh):
    in_specs = (
        P(("group", "req"), None),
        P("req", "tensor"),
        P("req", None, "tensor"),
        P("req", None, "tensor"),
        P("group"),
        P(("group", "req")),
    )
    out_specs = P(("group", "req"), "tensor")
    return jax.shard_map(
        functools.partial(per_device, mesh.shape["req"], mesh.shape["tensor"]),
        mesh=mesh,
        in_specs=in_specs,
        out_specs=out_specs,
        check_vma=False,
    )
```
